32 devices in a mesh: grp: 2 (over x), row: 16 (over z, y, core).
Axes of the slice: x: 2, y: 2, z: 4, core: 2. Of those that a mesh axis runs over, the one named last changes fastest.
Arguments:
- system: float32 [32768, 16384], P(('grp', 'row')), parts along dimension 0, may hold values from -150 to 150
- measured: float32 [32768, 512], P(('grp', 'row')), parts along dimension 0, may hold values from -24 to 24
- row_class: int32 [32768], P(('grp', 'row')), parts along dimension 0, may hold values from 0 to 7
- band_weight: float32 [16], P('grp'), parts along dimension 0, may hold values from 0.3 to 1.5
- order: int32 [32, 2], P(('grp', 'row')), parts along dimension 0, may hold values from 0 to 1, each once within a row
Outputs:
- reconstruction: float32 [1024, 16384], P(('grp', 'row')), parts along dimension 0
The draws below stay inside these ranges and needn't reach their ends.
There are 2 independent parts, one for each index of `grp`. The reference program is written for one: setup_inputs(seed, part) draws one part's arguments, and reference() takes and returns one part's arrays. A program takes and returns all parts, laid end to end along the dimension named above; each array names one. Nothing has to cross between parts.
All inputs are finite; a program needn't handle non-finite values.
Results may differ from the reference program's by a relative error of at most 0.0001.
Values sent between devices are 32-bit elements; how exact they have to be, the bound alone decides.
A program may use at most 128 MiB of HBM per device.

```python
import math
import jax
import jax.numpy as jnp
from jax import lax

M = 16384
V = 16384
BATCH_FRAMES = 32
STEPS = 6
SUBBLOCK_COUNT = 2
BANDS = 8
NBLK = 16
FRAMES = 512
N_ROW = 16


def draw_system(key, part):
    key_base, key_rows, key_cols = jax.random.split(key, 3)
    base = jnp.clip(jax.random.normal(key_base, (M, V), jnp.float32), -6.0, 6.0)
    lower = math.log(0.5)
    upper = math.log(5.0)
    row_scale = jnp.exp(jax.random.uniform(key_rows, (M, 1), jnp.float32, lower, upper))
    col_scale = jnp.exp(jax.random.uniform(key_cols, (1, V), jnp.float32, lower, upper))
    return base * row_scale * col_scale


def plant(result, own_key, least, top_value):
    index_at = [jax.random.randint(jax.random.fold_in(own_key, axis), (), 0, length) for axis, length in enumerate(result.shape)]
    main_axis = result.shape.index(max(result.shape))
    neighbour = index_at[:main_axis] + [(index_at[main_axis] + 1) % result.shape[main_axis]] + index_at[main_axis + 1:]
    return result.at[tuple(index_at)].set(least).at[tuple(neighbour)].set(top_value)


def shard_levels(rng, shape, shards, least, largest):
    def one(axis_at, shards_of):
        steps = jax.random.uniform(jax.random.fold_in(jax.random.fold_in(rng, 6), axis_at), (shards_of,), jnp.float32, least / len(shards), largest / len(shards))
        return jnp.repeat(jnp.exp(steps), shape[axis_at] // shards_of).reshape((-1,) + (1,) * (len(shape) - axis_at - 1))

    loudness = one(*shards[0])
    for cut in shards[1:]:
        loudness = loudness * one(*cut)
    return loudness


def scatter_about(stream_key, shape, width, reach, cuts=(), kind=jnp.bfloat16):
    result = width * jax.random.normal(stream_key, shape, jnp.float32)
    if cuts:
        result = result * shard_levels(stream_key, shape, cuts, -0.22, 0.18)
    return jnp.clip(result, -reach, reach).astype(kind)


def setup_inputs(seed: int = 0, part: int = 0) -> dict:
    key_list = jax.random.split(jax.random.key(seed), 6)
    part_keys = jax.random.split(jax.random.fold_in(key_list[5], part), 6)
    return {
        "system": draw_system(jax.random.fold_in(jax.random.fold_in(key_list[5], part), 71), part),
        "measured": scatter_about(part_keys[1], (M, FRAMES), 4.0, 24.0, ((0, 16),), jnp.float32),
        "row_class": plant(jax.random.randint(part_keys[2], (M,), 0, BANDS), jax.random.fold_in(part_keys[2], 1), 0, BANDS - 1).astype(jnp.int32),
        "band_weight": jnp.clip(jnp.exp(jax.random.uniform(part_keys[3], (BANDS,), jnp.float32, math.log(0.3), math.log(1.5))), 0.3, 1.5),
        "order": jax.vmap(lambda own: jax.random.permutation(own, SUBBLOCK_COUNT))(jax.random.split(part_keys[4], NBLK)).reshape((NBLK, SUBBLOCK_COUNT)).astype(jnp.int32),
    }


epsilon = 1e-6


def reference(system, measured, row_class, band_weight, order):
    total_blocks = N_ROW
    block_rows = M // total_blocks
    subblock_rows = block_rows // SUBBLOCK_COUNT
    band_hits = (row_class[:, None] == jnp.arange(BANDS, dtype=jnp.int32)[None, :]).astype(jnp.float32)
    row_weight = jnp.dot(band_hits, band_weight, precision=lax.Precision.HIGHEST) / (jnp.sum(system * system, axis=1) + epsilon)
    block_matrix = system.reshape(total_blocks, SUBBLOCK_COUNT, subblock_rows, V)
    block_weight = row_weight.reshape(total_blocks, SUBBLOCK_COUNT, subblock_rows)
    block_signal = measured.reshape(total_blocks, SUBBLOCK_COUNT, subblock_rows, total_blocks, BATCH_FRAMES)
    pictures = jnp.zeros((total_blocks, BATCH_FRAMES, V), jnp.float32)
    block_numbers = jnp.arange(total_blocks, dtype=jnp.int32)

    def visit(packed_values):
        local_matrix, local_weight, local_signal, local_ordering, particle_image = packed_values
        for which in range(SUBBLOCK_COUNT):
            selected_block = local_ordering[which]
            sub_matrix = local_matrix[selected_block]
            sub_weight = local_weight[selected_block]
            observed_signal = local_signal[selected_block]
            forward = jnp.einsum('fv,rv->fr', particle_image, sub_matrix, precision=lax.Precision.HIGHEST)
            residual = observed_signal.T - forward
            particle_image = jnp.maximum(particle_image + jnp.einsum('fr,rv->fv', residual * sub_weight[None, :], sub_matrix, precision=lax.Precision.HIGHEST), 0.0)
        return particle_image

    for visit_no in range(STEPS):
        block_holders = (block_numbers - visit_no) % total_blocks
        carried = pictures[block_holders]
        observed_full = block_signal[block_numbers, :, :, block_holders, :]
        carried = lax.map(visit, (block_matrix, block_weight, observed_full, order, carried))
        pictures = pictures.at[block_holders].set(carried)
    return pictures.reshape(total_blocks * BATCH_FRAMES, V)
```

```python
import functools

import jax
import jax.numpy as jnp
from jax import lax
from jax.experimental import pallas as pl
from jax.experimental.pallas import tpu as pltpu
from jax.sharding import PartitionSpec as P

BATCH_FRAMES = 32
STEPS = 6
TILE = 1024
PIECES = (4, 8, 4)
VMEM_BYTES = 40 * 1024 * 1024

epsilon = 1e-06


def two_parts(value):
    high = value.astype(jnp.bfloat16)
    low = (value - high.astype(jnp.float32)).astype(jnp.bfloat16)
    return high, low


def stacked_parts(image):
    high, low = two_parts(image)
    return jnp.concatenate([high, low, jnp.zeros((64, image.shape[1]), jnp.bfloat16)], axis=0)


def forward_product(matrix, parts):
    high, low = two_parts(matrix)
    dims = (((1,), (1,)), ((), ()))
    return lax.dot_general(
        high, parts, dims, preferred_element_type=jnp.float32
    ) + lax.dot_general(low, parts, dims, preferred_element_type=jnp.float32)


def update_product(weighted, matrix):
    high, low = two_parts(matrix)
    both = jnp.dot(weighted, high, preferred_element_type=jnp.float32)
    rest = jnp.dot(weighted[:BATCH_FRAMES], low, preferred_element_type=jnp.float32)
    return both[:BATCH_FRAMES] + both[BATCH_FRAMES:] + rest


def weighted_residual(signal, forward, weight):
    high, low = two_parts((signal - forward) * weight)
    return jnp.concatenate([high, low], axis=0)


def folded(total):
    turned = total.T
    return turned[:BATCH_FRAMES] + turned[BATCH_FRAMES : 2 * BATCH_FRAMES]


def first_kernel(scalars, signal, weight, weighted_out):
    weighted_out[...] = weighted_residual(signal[...], 0.0, weight[...])


def forward_kernel(first, last, *refs):
    refs = list(refs)[1:]
    matrix, image = refs[:2]
    rest = refs[2:]
    total_in = None if first else rest.pop(0)
    if last:
        signal, weight, out, total = rest
    else:
        (total,) = rest
    step = pl.program_id(0)

    @pl.when(step == 0)
    def _():
        total[...] = jnp.zeros_like(total) if first else total_in[...]

    total[...] += forward_product(matrix[...], stacked_parts(image[...]))

    if last:

        @pl.when(step == pl.num_programs(0) - 1)
        def _():
            out[...] = weighted_residual(signal[...], folded(total[...]), weight[...])


def middle_kernel(starts, *refs):
    refs = list(refs)[1:]
    old, new, weighted = refs[:3]
    pieces = refs[3 : 3 + len(starts)]
    signal, weight, image_out, weighted_out, total, parts = refs[3 + len(starts) :]
    step = pl.program_id(0)

    @pl.when(step == 0)
    def _():
        total[...] = jnp.zeros_like(total)
        parts[...] = jnp.zeros_like(parts)

    total[...] += forward_product(new[...], parts[...])
    change = update_product(weighted[...], old[...])
    if pieces:
        image = pieces[0][...]
        for start, piece in zip(starts[1:], pieces[1:]):
            image = jnp.where(step >= start, piece[...], image)
        change = image + change
    image = jnp.maximum(change, 0.0)
    image_out[...] = image
    parts[...] = stacked_parts(image)

    @pl.when(step == pl.num_programs(0) - 1)
    def _():
        weighted_out[...] = weighted_residual(signal[...], folded(total[...]), weight[...])


def last_kernel(scalars, matrix, weighted, image, *refs):
    image_out = refs[-1]
    image_out[...] = jnp.maximum(
        image[...] + update_product(weighted[...], matrix[...]), 0.0
    )


def called(kernel, grid, in_specs, out_specs, out_shape, scratch, flops, bytes_accessed):
    return pl.pallas_call(
        kernel,
        grid_spec=pltpu.PrefetchScalarGridSpec(
            num_scalar_prefetch=1,
            grid=(grid,),
            in_specs=in_specs,
            out_specs=out_specs,
            scratch_shapes=scratch,
        ),
        out_shape=out_shape,
        compiler_params=pltpu.CompilerParams(vmem_limit_bytes=VMEM_BYTES),
        cost_estimate=pl.CostEstimate(
            flops=flops, bytes_accessed=bytes_accessed, transcendentals=0
        ),
    )


def shifted(value, axis, steps):
    count = lax.axis_size(axis)
    pairs = [(source, (source + steps) % count) for source in range(count)]
    return lax.ppermute(value, axis, pairs)


def local(system, measured, row_class, band_weight, order):
    cycle_size = lax.axis_size("row")
    position = lax.axis_index("row")
    rows_here, voxels = system.shape
    rows = rows_here // order.shape[1]
    frames = BATCH_FRAMES
    tile = TILE
    tiles = voxels // tile
    counts = [share * tiles // sum(PIECES) for share in PIECES]
    starts = [sum(counts[:at]) for at in range(len(counts))]

    band_hits = (
        row_class[:, None] == jnp.arange(band_weight.shape[0], dtype=jnp.int32)[None, :]
    ).astype(jnp.float32)
    row_weight = jnp.dot(band_hits, band_weight, precision=lax.Precision.HIGHEST) / (
        jnp.sum(system * system, axis=1) + epsilon
    )
    row_weight = row_weight.reshape(-1, 1, rows)
    signals = measured.reshape(-1, rows, measured.shape[1]).transpose(0, 2, 1)

    f32, bf16 = jnp.float32, jnp.bfloat16
    weighted_shape = jax.ShapeDtypeStruct((2 * frames, rows), bf16)
    total_shape = jax.ShapeDtypeStruct((rows, 128), f32)
    total_scratch = pltpu.VMEM((rows, 128), f32)

    def matrix_spec(which, at):
        return pl.BlockSpec((rows, tile), lambda i, s: (s[which], at(i)))

    def signal_specs(which):
        return [
            pl.BlockSpec((None, frames, rows), lambda i, s: (s[which], s[2], 0)),
            pl.BlockSpec((None, 1, rows), lambda i, s: (s[which], 0, 0)),
        ]

    def whole_spec(shape):
        return pl.BlockSpec(shape, lambda i, s: (0, 0))

    weighted_spec = whole_spec((2 * frames, rows))
    total_spec = whole_spec((rows, 128))
    work = rows * tile
    moved = rows * tile // 4

    pieces = None
    for visit_no in range(STEPS):
        owner = (position - visit_no) % cycle_size
        scalars = jnp.stack([order[0, 0], order[0, 1], owner]).astype(jnp.int32)
        if pieces is None:
            weighted = called(
                first_kernel, 1, signal_specs(0), weighted_spec, weighted_shape, [], 1, 1
            )(scalars, signals, row_weight)
        else:
            total = None
            for at, (start, count) in enumerate(zip(starts, counts)):
                first, last = at == 0, at + 1 == len(counts)
                specs = [
                    matrix_spec(0, lambda i, start=start: start + i),
                    pl.BlockSpec((frames, tile), lambda i, s: (0, i)),
                ]
                values = [system, pieces[at]]
                if not first:
                    specs.append(total_spec)
                    values.append(total)
                if last:
                    specs += signal_specs(0)
                    values += [signals, row_weight]
                total = called(
                    functools.partial(forward_kernel, first, last),
                    count,
                    specs,
                    weighted_spec if last else total_spec,
                    weighted_shape if last else total_shape,
                    [total_scratch] if last else [],
                    work * count,
                    moved * count,
                )(scalars, *values)
            weighted = total

        inside = [] if pieces is None else pieces
        specs = [
            matrix_spec(0, lambda i: jnp.minimum(i, tiles - 1)),
            matrix_spec(1, lambda i: jnp.maximum(i - 1, 0)),
            weighted_spec,
        ]
        for start, count, _ in zip(starts, counts, inside):
            specs.append(
                pl.BlockSpec(
                    (frames, tile),
                    lambda i, s, start=start, count=count: (
                        0,
                        jnp.clip(i - start, 0, count - 1),
                    ),
                )
            )
        specs += signal_specs(1)
        image, weighted = called(
            functools.partial(middle_kernel, starts[: len(inside)]),
            tiles + 1,
            specs,
            [
                pl.BlockSpec((frames, tile), lambda i, s: (0, jnp.minimum(i, tiles - 1))),
                weighted_spec,
            ],
            [jax.ShapeDtypeStruct((frames, voxels), f32), weighted_shape],
            [total_scratch, pltpu.VMEM((128, tile), bf16)],
            2 * work * tiles,
            2 * moved * tiles,
        )(scalars, system, system, weighted, *inside, signals, row_weight)

        steps = 1 if visit_no + 1 < STEPS else 1 - STEPS
        pieces = []
        earlier = []
        for start, count in zip(starts, counts):
            piece = called(
                last_kernel,
                count,
                [
                    matrix_spec(1, lambda i, start=start: start + i),
                    weighted_spec,
                    pl.BlockSpec((frames, tile), lambda i, s, start=start: (0, start + i)),
                ]
                + [pl.BlockSpec(memory_space=pl.ANY)] * len(earlier),
                pl.BlockSpec((frames, tile), lambda i, s: (0, i)),
                jax.ShapeDtypeStruct((frames, count * tile), f32),
                [],
                work * count,
                moved * count,
            )(scalars, system, weighted, image, *earlier)
            earlier = [piece]
            pieces.append(shifted(piece, "row", steps))
    return jnp.concatenate(pieces, axis=1)


def solution(mesh):
    return jax.shard_map(
        local,
        mesh=mesh,
        in_specs=(
            P(("grp", "row"), None),
            P(("grp", "row"), None),
            P(("grp", "row")),
            P("grp"),
            P(("grp", "row"), None),
        ),
        out_specs=P(("grp", "row"), None),
        check_vma=False,
    )
```

```python
import functools

import jax
import jax.numpy as jnp
from jax import lax
from jax.experimental import pallas as pl
from jax.experimental.pallas import tpu as pltpu
from jax.sharding import PartitionSpec as P

BATCH_FRAMES = 32
STEPS = 6
TILE = 1024
PIECES = (5, 6, 5)
VMEM_BYTES = 40 * 1024 * 1024

epsilon = 1e-06


def two_parts(value):
    high = value.astype(jnp.bfloat16)
    low = (value - high.astype(jnp.float32)).astype(jnp.bfloat16)
    return high, low


def stacked_parts(image):
    high, low = two_parts(image)
    return jnp.concatenate([high, low, jnp.zeros((64, image.shape[1]), jnp.bfloat16)], axis=0)


def forward_product(matrix, parts):
    high, low = two_parts(matrix)
    dims = (((1,), (1,)), ((), ()))
    return lax.dot_general(
        high, parts, dims, preferred_element_type=jnp.float32
    ) + lax.dot_general(low, parts, dims, preferred_element_type=jnp.float32)


def update_product(weighted, matrix):
    high, low = two_parts(matrix)
    both = jnp.dot(weighted, high, preferred_element_type=jnp.float32)
    rest = jnp.dot(weighted[:BATCH_FRAMES], low, preferred_element_type=jnp.float32)
    return both[:BATCH_FRAMES] + both[BATCH_FRAMES:] + rest


def weighted_residual(signal, forward, weight):
    high, low = two_parts((signal - forward) * weight)
    return jnp.concatenate([high, low], axis=0)


def folded(total):
    turned = total.T
    return turned[:BATCH_FRAMES] + turned[BATCH_FRAMES : 2 * BATCH_FRAMES]


def first_kernel(scalars, signal, weight, weighted_out):
    weighted_out[...] = weighted_residual(signal[...], 0.0, weight[...])


def forward_kernel(last, *refs):
    matrix, image, total_in = refs[1:4]
    rest = refs[4:]
    if last:
        signal, weight, out, total = rest
    else:
        (total,) = rest
    step = pl.program_id(0)

    @pl.when(step == 0)
    def _():
        total[...] = total_in[...]

    total[...] += forward_product(matrix[...], stacked_parts(image[...]))

    if last:

        @pl.when(step == pl.num_programs(0) - 1)
        def _():
            out[...] = weighted_residual(signal[...], folded(total[...]), weight[...])


def middle_kernel(starts, *refs):
    refs = list(refs)[1:]
    old, new, weighted = refs[:3]
    pieces = refs[3 : 3 + len(starts)]
    signal, weight, image_out, weighted_out, total, parts = refs[3 + len(starts) :]
    step = pl.program_id(0)

    @pl.when(step == 0)
    def _():
        total[...] = jnp.zeros_like(total)
        parts[...] = jnp.zeros_like(parts)

    total[...] += forward_product(new[...], parts[...])
    change = update_product(weighted[...], old[...])
    if pieces:
        image = pieces[0][...]
        for start, piece in zip(starts[1:], pieces[1:]):
            image = jnp.where(step >= start, piece[...], image)
        change = image + change
    image = jnp.maximum(change, 0.0)
    image_out[...] = image
    parts[...] = stacked_parts(image)

    @pl.when(step == pl.num_programs(0) - 1)
    def _():
        weighted_out[...] = weighted_residual(signal[...], folded(total[...]), weight[...])


def last_kernel(scalars, matrix, weighted, image, *refs):
    image_out = refs[-1]
    image_out[...] = jnp.maximum(
        image[...] + update_product(weighted[...], matrix[...]), 0.0
    )


def crossing_kernel(scalars, old, new, weighted, image, arrived, image_out, total):
    @pl.when(pl.program_id(0) == 0)
    def _():
        total[...] = jnp.zeros_like(total)

    total[...] += forward_product(new[...], stacked_parts(arrived[...]))
    image_out[...] = jnp.maximum(image[...] + update_product(weighted[...], old[...]), 0.0)


def called(kernel, grid, in_specs, out_specs, out_shape, scratch, flops, bytes_accessed):
    return pl.pallas_call(
        kernel,
        grid_spec=pltpu.PrefetchScalarGridSpec(
            num_scalar_prefetch=1,
            grid=(grid,),
            in_specs=in_specs,
            out_specs=out_specs,
            scratch_shapes=scratch,
        ),
        out_shape=out_shape,
        compiler_params=pltpu.CompilerParams(vmem_limit_bytes=VMEM_BYTES),
        cost_estimate=pl.CostEstimate(
            flops=flops, bytes_accessed=bytes_accessed, transcendentals=0
        ),
    )


def shifted(value, axis, steps):
    count = lax.axis_size(axis)
    pairs = [(source, (source + steps) % count) for source in range(count)]
    return lax.ppermute(value, axis, pairs)


def local(system, measured, row_class, band_weight, order):
    cycle_size = lax.axis_size("row")
    position = lax.axis_index("row")
    rows_here, voxels = system.shape
    rows = rows_here // order.shape[1]
    frames = BATCH_FRAMES
    tile = TILE
    tiles = voxels // tile
    counts = [share * tiles // sum(PIECES) for share in PIECES]
    assert counts[0] == counts[-1] and sum(counts) == tiles
    starts = [sum(counts[:at]) for at in range(len(counts))]

    band_hits = (
        row_class[:, None] == jnp.arange(band_weight.shape[0], dtype=jnp.int32)[None, :]
    ).astype(jnp.float32)
    row_weight = jnp.dot(band_hits, band_weight, precision=lax.Precision.HIGHEST) / (
        jnp.sum(system * system, axis=1) + epsilon
    )
    row_weight = row_weight.reshape(-1, 1, rows)
    signals = measured.reshape(-1, rows, measured.shape[1]).transpose(0, 2, 1)

    f32, bf16 = jnp.float32, jnp.bfloat16
    weighted_shape = jax.ShapeDtypeStruct((2 * frames, rows), bf16)
    total_shape = jax.ShapeDtypeStruct((rows, 128), f32)
    total_scratch = pltpu.VMEM((rows, 128), f32)

    def matrix_spec(which, at):
        return pl.BlockSpec((rows, tile), lambda i, s: (s[which], at(i)))

    def signal_specs(which):
        return [
            pl.BlockSpec((None, frames, rows), lambda i, s: (s[which], s[2], 0)),
            pl.BlockSpec((None, 1, rows), lambda i, s: (s[which], 0, 0)),
        ]

    def whole_spec(shape):
        return pl.BlockSpec(shape, lambda i, s: (0, 0))

    weighted_spec = whole_spec((2 * frames, rows))
    total_spec = whole_spec((rows, 128))
    work = rows * tile
    moved = rows * tile // 4

    pieces = None
    for visit_no in range(STEPS):
        owner = (position - visit_no) % cycle_size
        scalars = jnp.stack([order[0, 0], order[0, 1], owner]).astype(jnp.int32)
        if pieces is None:
            weighted = called(
                first_kernel, 1, signal_specs(0), weighted_spec, weighted_shape, [], 1, 1
            )(scalars, signals, row_weight)
        else:
            for at in range(1, len(counts)):
                start, count = starts[at], counts[at]
                last = at + 1 == len(counts)
                specs = [
                    matrix_spec(0, lambda i, start=start: start + i),
                    pl.BlockSpec((frames, tile), lambda i, s: (0, i)),
                    total_spec,
                ]
                values = [system, pieces[at], total]
                if last:
                    specs += signal_specs(0)
                    values += [signals, row_weight]
                total = called(
                    functools.partial(forward_kernel, last),
                    count,
                    specs,
                    weighted_spec if last else total_spec,
                    weighted_shape if last else total_shape,
                    [total_scratch] if last else [],
                    work * count,
                    moved * count,
                )(scalars, *values)
            weighted = total

        inside = [] if pieces is None else pieces
        specs = [
            matrix_spec(0, lambda i: jnp.minimum(i, tiles - 1)),
            matrix_spec(1, lambda i: jnp.maximum(i - 1, 0)),
            weighted_spec,
        ]
        for start, count, _ in zip(starts, counts, inside):
            specs.append(
                pl.BlockSpec(
                    (frames, tile),
                    lambda i, s, start=start, count=count: (
                        0,
                        jnp.clip(i - start, 0, count - 1),
                    ),
                )
            )
        specs += signal_specs(1)
        image, weighted = called(
            functools.partial(middle_kernel, starts[: len(inside)]),
            tiles + 1,
            specs,
            [
                pl.BlockSpec((frames, tile), lambda i, s: (0, jnp.minimum(i, tiles - 1))),
                weighted_spec,
            ],
            [jax.ShapeDtypeStruct((frames, voxels), f32), weighted_shape],
            [total_scratch, pltpu.VMEM((128, tile), bf16)],
            2 * work * tiles,
            2 * moved * tiles,
        )(scalars, system, system, weighted, *inside, signals, row_weight)

        steps = 1 if visit_no + 1 < STEPS else 1 - STEPS
        pieces = []
        earlier = []
        for at, (start, count) in enumerate(zip(starts, counts)):
            if at + 1 == len(counts) and visit_no + 1 < STEPS:
                piece, total = called(
                    crossing_kernel,
                    count,
                    [
                        matrix_spec(1, lambda i, start=start: start + i),
                        matrix_spec(0, lambda i: i),
                        weighted_spec,
                        pl.BlockSpec((frames, tile), lambda i, s, start=start: (0, start + i)),
                        pl.BlockSpec((frames, tile), lambda i, s: (0, i)),
                    ],
                    [pl.BlockSpec((frames, tile), lambda i, s: (0, i)), total_spec],
                    [jax.ShapeDtypeStruct((frames, count * tile), f32), total_shape],
                    [],
                    2 * work * count,
                    2 * moved * count,
                )(scalars, system, system, weighted, image, pieces[0])
                pieces.append(shifted(piece, "row", steps))
                continue
            piece = called(
                last_kernel,
                count,
                [
                    matrix_spec(1, lambda i, start=start: start + i),
                    weighted_spec,
                    pl.BlockSpec((frames, tile), lambda i, s, start=start: (0, start + i)),
                ]
                + [pl.BlockSpec(memory_space=pl.ANY)] * len(earlier),
                pl.BlockSpec((frames, tile), lambda i, s: (0, i)),
                jax.ShapeDtypeStruct((frames, count * tile), f32),
                [],
                work * count,
                moved * count,
            )(scalars, system, weighted, image, *earlier)
            earlier = [piece]
            pieces.append(shifted(piece, "row", steps))
    return jnp.concatenate(pieces, axis=1)


def solution(mesh):
    return jax.shard_map(
        local,
        mesh=mesh,
        in_specs=(
            P(("grp", "row"), None),
            P(("grp", "row"), None),
            P(("grp", "row")),
            P("grp"),
            P(("grp", "row"), None),
        ),
        out_specs=P(("grp", "row"), None),
        check_vma=False,
    )
```

```python
import functools

import jax
import jax.numpy as jnp
from jax import lax
from jax.experimental import pallas as pl
from jax.experimental.pallas import tpu as pltpu
from jax.sharding import PartitionSpec as P

BATCH_FRAMES = 32
STEPS = 6
TILE = 1024
PIECES = (5, 6, 5)
VMEM_BYTES = 40 * 1024 * 1024

epsilon = 1e-06


def two_parts(value):
    high = value.astype(jnp.bfloat16)
    low = (value - high.astype(jnp.float32)).astype(jnp.bfloat16)
    return high, low


def stacked_parts(image):
    high, low = two_parts(image)
    return jnp.concatenate([high, low, jnp.zeros((64, image.shape[1]), jnp.bfloat16)], axis=0)


def forward_product(matrix, parts):
    high, low = two_parts(matrix)
    dims = (((1,), (1,)), ((), ()))
    return lax.dot_general(
        high, parts, dims, preferred_element_type=jnp.float32
    ) + lax.dot_general(low, parts, dims, preferred_element_type=jnp.float32)


def update_product(weighted, matrix):
    high, low = two_parts(matrix)
    both = jnp.dot(weighted, high, preferred_element_type=jnp.float32)
    rest = jnp.dot(weighted[:BATCH_FRAMES], low, preferred_element_type=jnp.float32)
    return both[:BATCH_FRAMES] + both[BATCH_FRAMES:] + rest


def weighted_residual(signal, forward, weight):
    high, low = two_parts((signal - forward) * weight)
    return jnp.concatenate([high, low], axis=0)


def folded(total):
    turned = total.T
    return turned[:BATCH_FRAMES] + turned[BATCH_FRAMES : 2 * BATCH_FRAMES]


def first_kernel(scalars, signal, weight, weighted_out):
    weighted_out[...] = weighted_residual(signal[...], 0.0, weight[...])


def forward_kernel(last, *refs):
    matrix, image, total_in = refs[1:4]
    rest = refs[4:]
    if last:
        signal, weight, out, total = rest
    else:
        (total,) = rest
    step = pl.program_id(0)

    @pl.when(step == 0)
    def _():
        total[...] = total_in[...]

    total[...] += forward_product(matrix[...], stacked_parts(image[...]))

    if last:

        @pl.when(step == pl.num_programs(0) - 1)
        def _():
            out[...] = weighted_residual(signal[...], folded(total[...]), weight[...])


def middle_kernel(starts, *refs):
    refs = list(refs)[1:]
    old, new, weighted = refs[:3]
    pieces = refs[3 : 3 + len(starts)]
    signal, weight, image_out, weighted_out, total, parts = refs[3 + len(starts) :]
    step = pl.program_id(0)

    @pl.when(step == 0)
    def _():
        total[...] = jnp.zeros_like(total)
        parts[...] = jnp.zeros_like(parts)

    total[...] += forward_product(new[...], parts[...])
    change = update_product(weighted[...], old[...])
    if pieces:
        image = pieces[0][...]
        for start, piece in zip(starts[1:], pieces[1:]):
            image = jnp.where(step >= start, piece[...], image)
        change = image + change
    image = jnp.maximum(change, 0.0)
    image_out[...] = image
    parts[...] = stacked_parts(image)

    @pl.when(step == pl.num_programs(0) - 1)
    def _():
        weighted_out[...] = weighted_residual(signal[...], folded(total[...]), weight[...])


def last_kernel(scalars, matrix, weighted, image, *refs):
    image_out = refs[-1]
    image_out[...] = jnp.maximum(
        image[...] + update_product(weighted[...], matrix[...]), 0.0
    )


def crossing_kernel(scalars, old, new, weighted, image, arrived, image_out, total):
    @pl.when(pl.program_id(0) == 0)
    def _():
        total[...] = jnp.zeros_like(total)

    total[...] += forward_product(new[...], stacked_parts(arrived[...]))
    image_out[...] = jnp.maximum(image[...] + update_product(weighted[...], old[...]), 0.0)


def called(kernel, grid, in_specs, out_specs, out_shape, scratch, flops, bytes_accessed):
    return pl.pallas_call(
        kernel,
        grid_spec=pltpu.PrefetchScalarGridSpec(
            num_scalar_prefetch=1,
            grid=(grid,),
            in_specs=in_specs,
            out_specs=out_specs,
            scratch_shapes=scratch,
        ),
        out_shape=out_shape,
        compiler_params=pltpu.CompilerParams(vmem_limit_bytes=VMEM_BYTES),
        cost_estimate=pl.CostEstimate(
            flops=flops, bytes_accessed=bytes_accessed, transcendentals=0
        ),
    )


def shifted(value, axis, steps):
    count = lax.axis_size(axis)
    pairs = [(source, (source + steps) % count) for source in range(count)]
    return lax.ppermute(value, axis, pairs)


def local(system, measured, row_class, band_weight, order):
    cycle_size = lax.axis_size("row")
    position = lax.axis_index("row")
    rows_here, voxels = system.shape
    rows = rows_here // order.shape[1]
    frames = BATCH_FRAMES
    tile = TILE
    tiles = voxels // tile
    counts = [share * tiles // sum(PIECES) for share in PIECES]
    assert counts[0] == counts[-1] and sum(counts) == tiles
    starts = [sum(counts[:at]) for at in range(len(counts))]

    band_hits = (
        row_class[:, None] == jnp.arange(band_weight.shape[0], dtype=jnp.int32)[None, :]
    ).astype(jnp.float32)
    row_weight = jnp.dot(band_hits, band_weight, precision=lax.Precision.HIGHEST) / (
        jnp.sum(system * system, axis=1) + epsilon
    )
    row_weight = row_weight.reshape(-1, 1, rows)
    signals = measured.reshape(-1, rows, measured.shape[1]).transpose(0, 2, 1)

    f32, bf16 = jnp.float32, jnp.bfloat16
    weighted_shape = jax.ShapeDtypeStruct((2 * frames, rows), bf16)
    total_shape = jax.ShapeDtypeStruct((rows, 128), f32)
    total_scratch = pltpu.VMEM((rows, 128), f32)

    def matrix_spec(which, at):
        return pl.BlockSpec((rows, tile), lambda i, s: (s[which], at(i)))

    def signal_specs(which):
        return [
            pl.BlockSpec((None, frames, rows), lambda i, s: (s[which], s[2], 0)),
            pl.BlockSpec((None, 1, rows), lambda i, s: (s[which], 0, 0)),
        ]

    def whole_spec(shape):
        return pl.BlockSpec(shape, lambda i, s: (0, 0))

    weighted_spec = whole_spec((2 * frames, rows))
    total_spec = whole_spec((rows, 128))
    work = rows * tile
    moved = rows * tile // 4

    pieces = None
    for visit_no in range(STEPS):
        owner = (position - visit_no) % cycle_size
        scalars = jnp.stack([order[0, 0], order[0, 1], owner]).astype(jnp.int32)
        if pieces is None:
            weighted = called(
                first_kernel, 1, signal_specs(0), weighted_spec, weighted_shape, [], 1, 1
            )(scalars, signals, row_weight)
        else:
            for at in range(1, len(counts)):
                start, count = starts[at], counts[at]
                last = at + 1 == len(counts)
                specs = [
                    matrix_spec(0, lambda i, start=start: start + i),
                    pl.BlockSpec((frames, tile), lambda i, s: (0, i)),
                    total_spec,
                ]
                values = [system, pieces[at], total]
                if last:
                    specs += signal_specs(0)
                    values += [signals, row_weight]
                total = called(
                    functools.partial(forward_kernel, last),
                    count,
                    specs,
                    weighted_spec if last else total_spec,
                    weighted_shape if last else total_shape,
                    [total_scratch] if last else [],
                    work * count,
                    moved * count,
                )(scalars, *values)
            weighted = total

        inside = [] if pieces is None else pieces
        specs = [
            matrix_spec(0, lambda i: jnp.minimum(i, tiles - 1)),
            matrix_spec(1, lambda i: jnp.maximum(i - 1, 0)),
            weighted_spec,
        ]
        for start, count, _ in zip(starts, counts, inside):
            specs.append(
                pl.BlockSpec(
                    (frames, tile),
                    lambda i, s, start=start, count=count: (
                        0,
                        jnp.clip(i - start, 0, count - 1),
                    ),
                )
            )
        specs += signal_specs(1)
        image, weighted = called(
            functools.partial(middle_kernel, starts[: len(inside)]),
            tiles + 1,
            specs,
            [
                pl.BlockSpec((frames, tile), lambda i, s: (0, jnp.minimum(i, tiles - 1))),
                weighted_spec,
            ],
            [jax.ShapeDtypeStruct((frames, voxels), f32), weighted_shape],
            [total_scratch, pltpu.VMEM((128, tile), bf16)],
            2 * work * tiles,
            2 * moved * tiles,
        )(scalars, system, system, weighted, *inside, signals, row_weight)

        steps = 1 if visit_no + 1 < STEPS else 1 - STEPS
        pieces = []
        earlier = []
        for at, (start, count) in enumerate(zip(starts, counts)):
            if at + 1 == len(counts) and visit_no + 1 < STEPS:
                piece, total = called(
                    crossing_kernel,
                    count,
                    [
                        matrix_spec(1, lambda i, start=start: start + i),
                        matrix_spec(0, lambda i: i),
                        weighted_spec,
                        pl.BlockSpec((frames, tile), lambda i, s, start=start: (0, start + i)),
                        pl.BlockSpec((frames, tile), lambda i, s: (0, i)),
                    ],
                    [pl.BlockSpec((frames, tile), lambda i, s: (0, i)), total_spec],
                    [jax.ShapeDtypeStruct((frames, count * tile), f32), total_shape],
                    [],
                    2 * work * count,
                    2 * moved * count,
                )(scalars, system, system, weighted, image, pieces[0])
                pieces.append(shifted(piece, "row", steps))
                continue
            piece = called(
                last_kernel,
                count,
                [
                    matrix_spec(1, lambda i, start=start: start + i),
                    weighted_spec,
                    pl.BlockSpec((frames, tile), lambda i, s, start=start: (0, start + i)),
                ]
                + [pl.BlockSpec(memory_space=pl.ANY)] * len(earlier),
                pl.BlockSpec((frames, tile), lambda i, s: (0, i)),
                jax.ShapeDtypeStruct((frames, count * tile), f32),
                [],
                work * count,
                moved * count,
            )(scalars, system, weighted, image, *earlier)
            pieces.append(shifted(piece, "row", steps))
            earlier = [piece] if at + 2 < len(counts) else [pieces[0]]
    return jnp.concatenate(pieces, axis=1)


def solution(mesh):
    return jax.shard_map(
        local,
        mesh=mesh,
        in_specs=(
            P(("grp", "row"), None),
            P(("grp", "row"), None),
            P(("grp", "row")),
            P("grp"),
            P(("grp", "row"), None),
        ),
        out_specs=P(("grp", "row"), None),
        check_vma=False,
    )
```
